32 devices in a mesh: pipe: 2 (over x), ctx: 8 (over z, core), tp: 2 (over y).
Axes of the slice: x: 2, y: 2, z: 4, core: 2. Of those that a mesh axis runs over, the one named last changes fastest.
Arguments:
- queries: bfloat16 [2, 512, 128, 128], P('pipe', 'ctx', 'tp'), may hold values from -10 to 10
- span_keys: bfloat16 [2, 512, 8, 128], P('pipe', 'ctx', 'tp'), may hold values from -6 to 6
- span_values: bfloat16 [2, 512, 8, 128], P('pipe', 'ctx', 'tp'), may hold values from -12 to 12
- cache_keys: bfloat16 [2, 256, 8, 128], P('pipe', 'ctx', 'tp'), may hold values from -6 to 6
- cache_values: bfloat16 [2, 256, 8, 128], P('pipe', 'ctx', 'tp'), may hold values from -6 to 6
- scale_exps: int32 [2, 16, 8, 2], P('pipe', 'ctx', 'tp'), may hold values from -3 to 1
- block_order: int32 [2, 16], P('pipe'), may hold values from 0 to 15, each once within a row
Outputs:
- handed: bfloat16 [2, 512, 128, 128], P('pipe', 'ctx', 'tp')
The draws below stay inside these ranges and needn't reach their ends.
All inputs are finite; a program needn't handle non-finite values.
Results may differ from the reference program's by a relative error of at most 0.006.
Values may be sent and summed in bfloat16 or wider, within the bound.
A program may use at most 128 MiB of HBM per device.

```python
import jax
import jax.numpy as jnp
from jax import lax

HEADS = 128
KVH = 8
HD = 128
CBLK = 16
GROUP = 16
SECTS = 2
HALF = 32
SPAN = 512
CTXT = 256
NBLK = 16
OWNERS = 16


def joint_draw(key):
    keys = jnp.clip(1.5 * jax.random.normal(jax.random.fold_in(key, 11), (SECTS, SPAN, KVH, HD), jnp.float32), -6.0, 6.0)
    query = jnp.clip(jax.random.normal(jax.random.fold_in(key, 12), (SECTS, SPAN, HEADS, HD), jnp.float32), -6.0, 6.0)
    return (query, keys)


def draw_queries(key, part):
    return joint_draw(key)[0].astype(jnp.bfloat16)


def draw_span_keys(key, part):
    return joint_draw(key)[1].astype(jnp.bfloat16)


def plant(values, key, least, largest):
    dims = values.shape
    place = [jax.random.randint(jax.random.fold_in(key, axis), (), 0, dims[axis]) for axis in range(len(dims))]
    values = values.at[tuple(place)].set(least)
    longest = dims.index(max(dims))
    place[longest] = (place[longest] + 1) % dims[longest]
    return values.at[tuple(place)].set(largest)


def level_of(stream_key, shape, shards, smallest, top_value):
    level, own = 1.0, jax.random.fold_in(stream_key, 6)
    for dim, parts in shards:
        draws = jnp.exp(jax.random.uniform(jax.random.fold_in(own, dim), (parts,), jnp.float32, smallest / len(shards), top_value / len(shards)))
        level = level * jnp.repeat(draws, shape[dim] // parts).reshape([-1 if axis == dim else 1 for axis in range(len(shape))])
    return level


def centred(key, shape, scale, limit, cuts=(), kind=jnp.bfloat16):
    array = jax.random.normal(key, shape, jnp.float32) * scale
    if len(cuts) > 0:
        array = level_of(key, shape, cuts, -0.22, 0.18) * array
    return jnp.clip(array, min=-limit, max=limit).astype(kind)


def setup_inputs(seed: int = 0) -> dict:
    key_list = jax.random.split(jax.random.key(seed), 8)
    queries = draw_queries(jax.random.fold_in(key_list[7], 71), 0)
    span_keys = draw_span_keys(jax.random.fold_in(key_list[7], 71), 0)
    span_values = centred(key_list[2], (SECTS, SPAN, KVH, HD), 2.0, 12.0, ((0, 2), (1, 8), (2, 2)))
    cache_keys = centred(key_list[3], (SECTS, CTXT, KVH, HD), 1.0, 6.0, ((0, 2), (1, 8), (2, 2)))
    cache_values = centred(key_list[4], (SECTS, CTXT, KVH, HD), 1.0, 6.0, ((0, 2), (1, 8), (2, 2)))
    scale_exps = plant(jax.random.randint(key_list[5], (SECTS, NBLK, KVH, 2), -3, 2), jax.random.fold_in(key_list[5], 1), -3, 1).astype(jnp.int32)
    block_order = jax.vmap(lambda own: jax.random.permutation(own, OWNERS))(jax.random.split(key_list[6], SECTS)).reshape((SECTS, OWNERS)).astype(jnp.int32)
    return dict(queries=queries, span_keys=span_keys, span_values=span_values, cache_keys=cache_keys, cache_values=cache_values, scale_exps=scale_exps, block_order=block_order)


def hadamard(order):
    rows = jnp.arange(order, dtype=jnp.int32)[:, None]
    cols = jnp.arange(order, dtype=jnp.int32)[None, :]
    common = jnp.zeros((order, order), jnp.int32)
    for bit in range(order.bit_length() - 1):
        common = common + (jnp.right_shift(rows, bit) & 1) * (jnp.right_shift(cols, bit) & 1)
    signs = 1.0 - 2.0 * (common % 2).astype(jnp.float32)
    return signs * (1.0 / (order ** 0.5))


def section(query, ckeys, cvalues, kcache, vcache, exps, order):
    factor = jnp.repeat(jnp.exp2(exps.astype(jnp.float32)), CBLK, axis=0)
    keys_ctx = (kcache.astype(jnp.float32) * factor[:, :, 0:1]).astype(jnp.bfloat16)
    vals_ctx = (vcache.astype(jnp.float32) * factor[:, :, 1:2]).astype(jnp.bfloat16)
    keys = jnp.concatenate([keys_ctx, ckeys], axis=0)
    vals = jnp.concatenate([vals_ctx, cvalues], axis=0)
    count = query.shape[0]
    index = jnp.arange(count, dtype=jnp.int32)
    position = order[index // HALF] * HALF + index % HALF
    visible = jnp.concatenate([jnp.ones((count, CTXT), bool), position[None, :] <= position[:, None]], axis=1)
    grouped = query.reshape(count, KVH, GROUP, HD)
    inv = 1.0 / (HD ** 0.5)

    def one_head(head):
        qhead = grouped[:, head].astype(jnp.float32)
        khead = keys[:, head].astype(jnp.float32)
        vhead = vals[:, head].astype(jnp.float32)
        score = jnp.einsum('tqd,kd->qtk', qhead, khead) * inv
        score = jnp.where(visible[None], score, -jnp.inf)
        top = jnp.max(score, axis=-1, keepdims=True)
        expo = jnp.exp(score - top)
        total = jnp.sum(expo, axis=-1)
        weight = expo.astype(jnp.bfloat16).astype(jnp.float32)
        return jnp.einsum('qtk,kd->qtd', weight, vhead) / total[..., None]

    mixed = lax.map(one_head, jnp.arange(KVH, dtype=jnp.int32))
    rotated = jnp.dot(mixed.reshape(-1, HD), hadamard(HD), precision=lax.Precision.HIGHEST)
    rotated = rotated.reshape(KVH, GROUP, count, HD).transpose(2, 0, 1, 3)
    return rotated.reshape(count, HEADS, HD).astype(jnp.bfloat16)


def reference(queries, span_keys, span_values, cache_keys, cache_values, scale_exps, block_order):
    outs = []
    for sect in range(SECTS):
        outs.append(section(queries[sect], span_keys[sect], span_values[sect], cache_keys[sect], cache_values[sect], scale_exps[sect], block_order[sect]))
    result = jnp.stack(outs, axis=0)
    return jnp.roll(result, 1, axis=0)
```

```python
import functools
import math

import jax
import jax.numpy as jnp
from jax import lax
from jax.experimental import pallas as pl
from jax.experimental.pallas import tpu as pltpu
from jax.sharding import PartitionSpec as P

CBLK = 16
LANES = 128
HIDDEN = -1e30
TILE_TOKENS = 16


def hadamard_signs(order):
    rows = lax.broadcasted_iota(jnp.int32, (order, order), 0)
    both = rows & lax.broadcasted_iota(jnp.int32, (order, order), 1)
    common = jnp.zeros((order, order), jnp.int32)
    for bit in range(order.bit_length() - 1):
        common = common + (jnp.right_shift(both, bit) & 1)
    return (1 - 2 * (common & 1)).astype(jnp.float32).astype(jnp.bfloat16)


def power_of_two(exponent):
    value = jnp.float32(2.0)
    for candidate in range(-3, 1):
        value = jnp.where(exponent == candidate, jnp.float32(2.0**candidate), value)
    return value


def kernel(
    sections, owners, q_ref, sk_ref, sv_ref, ck_ref, cv_ref, exps_ref, order_ref, out_ref,
    raw_span, raw_ctx, wide, stage, kv_far, kv_near, q_far, q_near, mixed, order_near, order_far, bias,
    load_sem, near_sem, ring_send, ring_recv, pair_send, pair_recv, query_send, query_recv,
    result_send, result_recv, store_sem,
):
    pipe, mine = lax.axis_index("pipe"), lax.axis_index("ctx")
    onward = lax.rem(pipe + 1, sections)
    before = lax.rem(pipe + sections - 1, sections)
    chips = owners // 2
    chip, core = lax.div(mine, 2), lax.rem(mine, 2)
    twin = chip * 2 + 1 - core
    tokens = q_ref.shape[1]
    kv_local = sk_ref.shape[2]
    group = q_ref.shape[2] // kv_local
    width = q_ref.shape[3]
    cache_len = ck_ref.shape[1]
    rows_dev = cache_len + tokens
    half = tokens // 2
    far_heads = kv_far.shape[0]
    near_heads = kv_near.shape[0]
    slot = pl.ds(pl.multiple_of(mine * rows_dev, 16), rows_dev)

    loads = [
        pltpu.make_async_copy(sk_ref.at[0], raw_span.at[0], load_sem.at[0]),
        pltpu.make_async_copy(sv_ref.at[0], raw_span.at[1], load_sem.at[1]),
        pltpu.make_async_copy(ck_ref.at[0], raw_ctx.at[0], load_sem.at[2]),
        pltpu.make_async_copy(cv_ref.at[0], raw_ctx.at[1], load_sem.at[3]),
    ]
    for load in loads:
        load.start()

    def heads(kv_head):
        return pl.ds(kv_head * group, group)

    barrier = pltpu.get_barrier_semaphore()
    pl.semaphore_signal(barrier, inc=1, device_id={"pipe": onward})
    greeted = 2
    if sections > 2:
        pl.semaphore_signal(barrier, inc=1, device_id={"pipe": before})
        greeted = 3
    pl.semaphore_signal(barrier, inc=1, device_id={"ctx": twin})

    @pl.when(chip > 0)
    def _():
        pl.semaphore_signal(barrier, inc=1, device_id={"ctx": mine - 2})

    @pl.when(chip < chips - 1)
    def _():
        pl.semaphore_signal(barrier, inc=1, device_id={"ctx": mine + 2})

    signs = hadamard_signs(width)
    for block in range(2 * owners):
        order_near[block : block + 1, :] = jnp.full((1, LANES), order_ref[0, block], jnp.int32)

    for neighbour in (chip > 0, chip < chips - 1):
        greeted = greeted + neighbour.astype(jnp.int32)
    pl.semaphore_wait(barrier, greeted)

    query_sends = [
        pltpu.make_async_remote_copy(
            q_ref.at[0, :, heads(head), :], q_far.at[head], query_send.at[head], query_recv.at[head],
            device_id={"pipe": onward},
        )
        for head in range(far_heads)
    ]
    query_sends[0].start()
    near_loads = [
        pltpu.make_async_copy(q_ref.at[0, :, heads(far_heads + head), :], q_near.at[head], near_sem.at[head])
        for head in range(near_heads)
    ]

    for load in loads:
        load.wait()
    for kind in range(2):
        wide[kind, :cache_len] = raw_ctx[kind].astype(jnp.float32)
        wide[kind, cache_len:] = raw_span[kind].astype(jnp.float32)

    def prepared(kv_head, kind):
        rows = wide[kind, :, kv_head, :]
        parts = [
            rows[block * CBLK : (block + 1) * CBLK] * power_of_two(exps_ref[0, block, kv_head, kind])
            for block in range(cache_len // CBLK)
        ]
        rows = jnp.concatenate(parts + [rows[cache_len:]], axis=0).astype(jnp.bfloat16)
        if kind == 1:
            rows = jnp.dot(rows, signs, preferred_element_type=jnp.float32).astype(jnp.bfloat16)
        return rows

    def block_copy(which, way, owner, target):
        held = (kv_far, kv_near)[which]
        part = held.at[:, :, pl.ds(pl.multiple_of(owner * rows_dev, 16), rows_dev), :]
        return pltpu.make_async_remote_copy(
            part, part, ring_send.at[which, way, owner], ring_recv.at[which, owner], device_id={"ctx": target}
        )

    def move(which, owner, way, act):
        target = (mine + 2, mine - 2, twin)[way]
        if way == 2:
            act(block_copy(which, way, owner, target))
        else:

            @pl.when((chip < chips - 1) if way == 0 else (chip > 0))
            def _():
                act(block_copy(which, way, owner, target))

    def send(copy):
        copy.start()

    def sent(copy):
        copy.wait_send()

    def own_block(which, act):
        for way in range(3):
            move(which, mine, way, act)

    def step(which, distance, act, waiting):
        for way, there, owner in (
            (0, chip >= distance, mine - 2 * distance),
            (1, chip + distance < chips, mine + 2 * distance),
        ):

            @pl.when(there)
            def _():
                if waiting:
                    block_copy(which, 2, owner, twin).wait_recv()
                move(which, owner, way, act)
                move(which, owner, 2, act)

    def twin_blocks(which):
        for other in range(chips):
            block_copy(which, 2, 2 * other + 1 - core, twin).wait_recv()

    for head in range(near_heads):
        for kind in range(2):
            kv_near[head, kind, slot, :] = prepared(far_heads + head, kind)
    own_block(1, send)
    for load in near_loads:
        load.start()
    for head in range(far_heads):
        for kind in range(2):
            stage[head, kind] = prepared(head, kind)
    pair_sends = [
        pltpu.make_async_remote_copy(
            stage, kv_far.at[:, :, slot, :], pair_send.at[0], pair_recv.at[0], device_id={"pipe": onward}
        ),
        pltpu.make_async_remote_copy(
            order_near, order_far, pair_send.at[1], pair_recv.at[1], device_id={"pipe": onward}
        ),
    ]
    for copy in pair_sends:
        copy.start()
    for copy in query_sends[1:]:
        copy.start()

    def fill_bias(order):
        token = lax.div(lax.broadcasted_iota(jnp.int32, (tokens * group, LANES), 0), group)
        first = order[pl.ds(2 * mine, 1), :]
        second = order[pl.ds(2 * mine + 1, 1), :]
        place = jnp.where(token < half, first, second) * half + lax.rem(token, half)
        for tile in range(owners * rows_dev // LANES):
            column = tile * LANES + lax.broadcasted_iota(jnp.int32, (1, LANES), 1)
            key_place = jnp.full((1, LANES), -1, jnp.int32)
            for block in range(2 * owners):
                start = (block // 2) * rows_dev + cache_len + (block % 2) * half
                if start < (tile + 1) * LANES and start + half > tile * LANES:
                    inside = (column >= start) & (column < start + half)
                    key_place = jnp.where(inside, order[block : block + 1, :] * half + column - start, key_place)
            bias[:, tile * LANES : (tile + 1) * LANES] = jnp.where(key_place <= place, 0.0, HIDDEN)

    scale = math.log2(math.e) / width**0.5
    shrink = 1.0 / width**0.5
    rows_tile = TILE_TOKENS * group

    def attend(queries, held, head, target):
        @pl.loop(0, tokens // TILE_TOKENS)
        def _(tile):
            part = pl.ds(pl.multiple_of(tile * TILE_TOKENS, TILE_TOKENS), TILE_TOKENS)
            rows = pl.ds(pl.multiple_of(tile * rows_tile, rows_tile), rows_tile)
            query = queries[head, part].reshape(rows_tile, width)
            score = lax.dot_general(
                query, held[head, 0], (((1,), (1,)), ((), ())), preferred_element_type=jnp.float32
            )
            score = score * scale + bias[rows, :]
            top = jnp.max(score, axis=-1, keepdims=True)
            weight = jnp.exp2(score - top).astype(jnp.bfloat16)
            values = held[head, 1]
            both = jnp.concatenate([values, jnp.ones_like(values)], axis=1)
            total = jnp.dot(weight, both, preferred_element_type=jnp.float32)
            result = total[:, :width] * (shrink / total[:, width:])
            mixed[target, part] = result.astype(jnp.bfloat16).reshape(TILE_TOKENS, group, width)

    fill_bias(order_near)
    step(1, 1, send, True)
    pair_sends[0].wait_recv()
    own_block(0, send)
    for distance in range(2, chips):
        step(1, distance, send, True)
    twin_blocks(1)
    pending = list(range(1, chips))
    result_sends = []
    for head in range(near_heads):
        if pending:
            step(0, pending.pop(0), send, True)
        near_loads[head].wait()
        attend(q_near, kv_near, head, far_heads + head)
        copy = pltpu.make_async_remote_copy(
            mixed.at[far_heads + head], out_ref.at[0, :, heads(far_heads + head), :],
            result_send.at[head], result_recv.at[head], device_id={"pipe": onward},
        )
        copy.start()
        result_sends.append(copy)
    for distance in pending:
        step(0, distance, send, True)
    pair_sends[1].wait_recv()
    fill_bias(order_far)
    twin_blocks(0)
    stores = []
    for head in range(far_heads):
        query_sends[head].wait_recv()
        attend(q_far, kv_far, head, head)
        copy = pltpu.make_async_copy(mixed.at[head], out_ref.at[0, :, heads(head), :], store_sem.at[head])
        copy.start()
        stores.append(copy)

    for which in range(2):
        own_block(which, sent)
        for distance in range(1, chips):
            step(which, distance, sent, False)
    for copy in pair_sends + query_sends:
        copy.wait_send()
    for copy in stores:
        copy.wait()
    for copy in result_sends:
        copy.wait()


def on_device(queries, span_keys, span_values, cache_keys, cache_values, scale_exps, block_order):
    sections, owners = lax.axis_size("pipe"), lax.axis_size("ctx")
    tokens, head_local, width = queries.shape[1:]
    kv_local = span_keys.shape[2]
    group = head_local // kv_local
    cache_len = cache_keys.shape[1]
    rows_dev = cache_len + tokens
    far, near = kv_local // 2, kv_local - kv_local // 2
    anywhere = pl.BlockSpec(memory_space=pl.ANY)
    scalars = pl.BlockSpec(memory_space=pltpu.SMEM)
    dma = pltpu.SemaphoreType.DMA
    return pl.pallas_call(
        functools.partial(kernel, sections, owners),
        out_shape=jax.ShapeDtypeStruct(queries.shape, jnp.bfloat16),
        in_specs=[anywhere] * 5 + [scalars] * 2,
        out_specs=anywhere,
        scratch_shapes=[
            pltpu.VMEM((2, tokens, kv_local, width), jnp.bfloat16),
            pltpu.VMEM((2, cache_len, kv_local, width), jnp.bfloat16),
            pltpu.VMEM((2, rows_dev, kv_local, width), jnp.float32),
            pltpu.VMEM((far, 2, rows_dev, width), jnp.bfloat16),
            pltpu.VMEM((far, 2, owners * rows_dev, width), jnp.bfloat16),
            pltpu.VMEM((near, 2, owners * rows_dev, width), jnp.bfloat16),
            pltpu.VMEM((far, tokens, group, width), jnp.bfloat16),
            pltpu.VMEM((near, tokens, group, width), jnp.bfloat16),
            pltpu.VMEM((kv_local, tokens, group, width), jnp.bfloat16),
            pltpu.VMEM((2 * owners, LANES), jnp.int32),
            pltpu.VMEM((2 * owners, LANES), jnp.int32),
            pltpu.VMEM((tokens * group, owners * rows_dev), jnp.float32),
            dma((4,)),
            dma((near,)),
            dma((2, 3, owners)),
            dma((2, owners)),
            dma((2,)),
            dma((2,)),
            dma((far,)),
            dma((far,)),
            dma((near,)),
            dma((near,)),
            dma((far,)),
        ],
        compiler_params=pltpu.CompilerParams(
            collective_id=0, has_side_effects=True, vmem_limit_bytes=48 * 1024 * 1024
        ),
    )(queries, span_keys, span_values, cache_keys, cache_values, scale_exps, block_order)


def solution(mesh):
    placed = P("pipe", "ctx", "tp", None)
    return jax.shard_map(
        on_device,
        mesh=mesh,
        in_specs=(placed,) * 6 + (P("pipe", None),),
        out_specs=placed,
        check_vma=False,
    )
```

```python
import functools
import math

import jax
import jax.numpy as jnp
from jax import lax
from jax.experimental import pallas as pl
from jax.experimental.pallas import tpu as pltpu
from jax.sharding import PartitionSpec as P

CBLK = 16
LANES = 128
HIDDEN = -1e30
TILE_TOKENS = 16
REACH = 2


def hadamard_signs(order):
    rows = lax.broadcasted_iota(jnp.int32, (order, order), 0)
    both = rows & lax.broadcasted_iota(jnp.int32, (order, order), 1)
    common = jnp.zeros((order, order), jnp.int32)
    for bit in range(order.bit_length() - 1):
        common = common + (jnp.right_shift(both, bit) & 1)
    return (1 - 2 * (common & 1)).astype(jnp.float32).astype(jnp.bfloat16)


def power_of_two(exponent):
    value = jnp.float32(2.0)
    for candidate in range(-3, 1):
        value = jnp.where(exponent == candidate, jnp.float32(2.0**candidate), value)
    return value


def kernel(
    sections, owners, q_ref, sk_ref, sv_ref, ck_ref, cv_ref, exps_ref, order_ref, out_ref,
    raw_span, raw_ctx, wide, stage, kv_far, kv_near, q_far, q_near, mixed, order_near, order_far, bias,
    load_sem, near_sem, far_send, far_recv, near_send, near_recv, pair_send, pair_recv, query_send, query_recv,
    result_send, result_recv, store_sem,
):
    pipe, mine = lax.axis_index("pipe"), lax.axis_index("ctx")
    onward = lax.rem(pipe + 1, sections)
    before = lax.rem(pipe + sections - 1, sections)
    chips = owners // 2
    chip, core = lax.div(mine, 2), lax.rem(mine, 2)
    twin = chip * 2 + 1 - core
    tokens = q_ref.shape[1]
    kv_local = sk_ref.shape[2]
    group = q_ref.shape[2] // kv_local
    width = q_ref.shape[3]
    cache_len = ck_ref.shape[1]
    rows_dev = cache_len + tokens
    half = tokens // 2
    far_heads = kv_far.shape[0]
    near_heads = kv_near.shape[0]
    slot = pl.ds(pl.multiple_of(mine * rows_dev, 16), rows_dev)

    loads = [
        pltpu.make_async_copy(sk_ref.at[0], raw_span.at[0], load_sem.at[0]),
        pltpu.make_async_copy(sv_ref.at[0], raw_span.at[1], load_sem.at[1]),
        pltpu.make_async_copy(ck_ref.at[0], raw_ctx.at[0], load_sem.at[2]),
        pltpu.make_async_copy(cv_ref.at[0], raw_ctx.at[1], load_sem.at[3]),
    ]
    for load in loads:
        load.start()

    def heads(kv_head):
        return pl.ds(kv_head * group, group)

    barrier = pltpu.get_barrier_semaphore()
    pl.semaphore_signal(barrier, inc=1, device_id={"pipe": onward})
    greeted = 2
    if sections > 2:
        pl.semaphore_signal(barrier, inc=1, device_id={"pipe": before})
        greeted = 3
    for distance in range(1, min(REACH, chips - 1) + 1):
        for near_enough in (chip >= distance, chip + distance < chips):
            greeted = greeted + near_enough.astype(jnp.int32)
    pl.semaphore_signal(barrier, inc=1, device_id={"ctx": twin})

    for distance in range(1, min(REACH, chips - 1) + 1):
        for there, other in ((chip >= distance, mine - 2 * distance), (chip + distance < chips, mine + 2 * distance)):

            @pl.when(there)
            def _():
                pl.semaphore_signal(barrier, inc=1, device_id={"ctx": other})

    signs = hadamard_signs(width)
    for block in range(2 * owners):
        order_near[block : block + 1, :] = jnp.full((1, LANES), order_ref[0, block], jnp.int32)

    pl.semaphore_wait(barrier, greeted)

    query_sends = [
        pltpu.make_async_remote_copy(
            q_ref.at[0, :, heads(head), :], q_far.at[head], query_send.at[head], query_recv.at[head],
            device_id={"pipe": onward},
        )
        for head in range(far_heads)
    ]
    near_loads = [
        pltpu.make_async_copy(q_ref.at[0, :, heads(far_heads + head), :], q_near.at[head], near_sem.at[head])
        for head in range(near_heads)
    ]

    for load in loads:
        load.wait()
    for kind in range(2):
        wide[kind, :cache_len] = raw_ctx[kind].astype(jnp.float32)
        wide[kind, cache_len:] = raw_span[kind].astype(jnp.float32)

    def prepared(kv_head, kind):
        rows = wide[kind, :, kv_head, :]
        parts = [
            rows[block * CBLK : (block + 1) * CBLK] * power_of_two(exps_ref[0, block, kind, kv_head])
            for block in range(cache_len // CBLK)
        ]
        rows = jnp.concatenate(parts + [rows[cache_len:]], axis=0).astype(jnp.bfloat16)
        if kind == 1:
            rows = jnp.dot(rows, signs, preferred_element_type=jnp.float32).astype(jnp.bfloat16)
        return rows

    def block_copy(which, head, way, owner, target):
        held = (kv_far, kv_near)[which]
        part = held.at[head, :, pl.ds(pl.multiple_of(owner * rows_dev, 16), rows_dev), :]
        return pltpu.make_async_remote_copy(
            part,
            part,
            (far_send, near_send)[which].at[head, way],
            (far_recv, near_recv)[which].at[head, owner],
            device_id={"ctx": target},
        )

    def others(distance):
        return (
            (chip + distance < chips, mine + 2 * distance, distance),
            (chip >= distance, mine - 2 * distance, chips + distance),
        )

    def send(copy):
        copy.start()

    def sent(copy):
        copy.wait_send()

    def own_head(which, head, act):
        for distance in range(min(REACH, chips - 1), 0, -1):
            for there, other, way in others(distance):

                @pl.when(there)
                def _():
                    act(block_copy(which, head, way, mine, other))

        act(block_copy(which, head, 0, mine, twin))

    def own_block(which, act):
        for head in range((far_heads, near_heads)[which]):
            own_head(which, head, act)

    def step(which, distance, act, waiting):
        ahead = ((chip > 0, mine - 2), (chip < chips - 1, mine + 2))
        for (there, other, way), (further, following) in zip(others(distance), ahead):
            for head in range((far_heads, near_heads)[which]):

                @pl.when(there)
                def _():
                    if waiting:
                        block_copy(which, head, 0, other, twin).wait_recv()

                if distance >= REACH:

                    @pl.when(there & further)
                    def _():
                        act(block_copy(which, head, 4 * chips + way, other, following))

                @pl.when(there)
                def _():
                    act(block_copy(which, head, 2 * chips + way, other, twin))

    def twin_blocks(which):
        for other in range(chips):
            for head in range((far_heads, near_heads)[which]):
                block_copy(which, head, 0, 2 * other + 1 - core, twin).wait_recv()

    for head in range(near_heads):
        for kind in range(2):
            kv_near[head, kind, slot, :] = prepared(far_heads + head, kind)
        own_head(1, head, send)
    for load in near_loads:
        load.start()
    for head in range(far_heads):
        for kind in range(2):
            stage[head, kind] = prepared(head, kind)
    pair_sends = [
        pltpu.make_async_remote_copy(
            stage, kv_far.at[:, :, slot, :], pair_send.at[0], pair_recv.at[0], device_id={"pipe": onward}
        ),
        pltpu.make_async_remote_copy(
            order_near, order_far, pair_send.at[1], pair_recv.at[1], device_id={"pipe": onward}
        ),
    ]
    for copy in pair_sends:
        copy.start()
    for copy in query_sends:
        copy.start()

    def fill_bias(order):
        token = lax.div(lax.broadcasted_iota(jnp.int32, (tokens * group, LANES), 0), group)
        first = order[pl.ds(2 * mine, 1), :]
        second = order[pl.ds(2 * mine + 1, 1), :]
        place = jnp.where(token < half, first, second) * half + lax.rem(token, half)
        for tile in range(owners * rows_dev // LANES):
            column = tile * LANES + lax.broadcasted_iota(jnp.int32, (1, LANES), 1)
            key_place = jnp.full((1, LANES), -1, jnp.int32)
            for block in range(2 * owners):
                start = (block // 2) * rows_dev + cache_len + (block % 2) * half
                if start < (tile + 1) * LANES and start + half > tile * LANES:
                    inside = (column >= start) & (column < start + half)
                    key_place = jnp.where(inside, order[block : block + 1, :] * half + column - start, key_place)
            bias[:, tile * LANES : (tile + 1) * LANES] = jnp.where(key_place <= place, 0.0, HIDDEN)

    scale = math.log2(math.e) / width**0.5
    shrink = 1.0 / width**0.5
    rows_tile = TILE_TOKENS * group

    def attend(queries, held, head, target, done=None):
        @pl.loop(0, tokens // TILE_TOKENS)
        def _(tile):
            part = pl.ds(pl.multiple_of(tile * TILE_TOKENS, TILE_TOKENS), TILE_TOKENS)
            rows = pl.ds(pl.multiple_of(tile * rows_tile, rows_tile), rows_tile)
            query = queries[head, part].reshape(rows_tile, width)
            score = lax.dot_general(
                query, held[head, 0], (((1,), (1,)), ((), ())), preferred_element_type=jnp.float32
            )
            score = score * scale + bias[rows, :]
            top = jnp.max(score, axis=-1, keepdims=True)
            weight = jnp.exp2(score - top).astype(jnp.bfloat16)
            values = held[head, 1]
            both = jnp.concatenate([values, jnp.ones_like(values)], axis=1)
            total = jnp.dot(weight, both, preferred_element_type=jnp.float32)
            result = total[:, :width] * (shrink / total[:, width:])
            mixed[target, part] = result.astype(jnp.bfloat16).reshape(TILE_TOKENS, group, width)
            if done is not None:
                done(tile)

    fill_bias(order_near)
    if chips > REACH:
        step(1, REACH, send, True)
    pair_sends[0].wait_recv()
    own_block(0, send)
    for distance in list(range(1, min(REACH, chips))) + list(range(REACH + 1, chips)):
        step(1, distance, send, True)
    twin_blocks(1)
    pending = [distance for distance in range(REACH, chips)] + list(range(1, min(REACH, chips)))

    def result_copy(head, tile):
        part = pl.ds(pl.multiple_of(tile * TILE_TOKENS, TILE_TOKENS), TILE_TOKENS)
        return pltpu.make_async_remote_copy(
            mixed.at[far_heads + head, part], out_ref.at[0, part, heads(far_heads + head), :],
            result_send.at[head, tile], result_recv.at[head, tile], device_id={"pipe": onward},
        )

    for head in range(near_heads):
        near_loads[head].wait()
        attend(q_near, kv_near, head, far_heads + head, lambda tile: result_copy(head, tile).start())
        if pending:
            step(0, pending.pop(0), send, True)
    for distance in pending:
        step(0, distance, send, True)
    pair_sends[1].wait_recv()
    fill_bias(order_far)
    twin_blocks(0)
    stores = []
    for head in range(far_heads):
        query_sends[head].wait_recv()
        attend(q_far, kv_far, head, head)
        copy = pltpu.make_async_copy(mixed.at[head], out_ref.at[0, :, heads(head), :], store_sem.at[head])
        copy.start()
        stores.append(copy)

    for which in range(2):
        own_block(which, sent)
        for distance in range(1, chips):
            step(which, distance, sent, False)
    for copy in pair_sends + query_sends:
        copy.wait_send()
    for copy in stores:
        copy.wait()
    for head in range(near_heads):
        for tile in range(tokens // TILE_TOKENS):
            result_copy(head, tile).wait()


def on_device(queries, span_keys, span_values, cache_keys, cache_values, scale_exps, block_order):
    sections, owners = lax.axis_size("pipe"), lax.axis_size("ctx")
    tokens, head_local, width = queries.shape[1:]
    kv_local = span_keys.shape[2]
    group = head_local // kv_local
    cache_len = cache_keys.shape[1]
    rows_dev = cache_len + tokens
    far, near = kv_local // 2, kv_local - kv_local // 2
    anywhere = pl.BlockSpec(memory_space=pl.ANY)
    scalars = pl.BlockSpec(memory_space=pltpu.SMEM)
    dma = pltpu.SemaphoreType.DMA
    return pl.pallas_call(
        functools.partial(kernel, sections, owners),
        out_shape=jax.ShapeDtypeStruct(queries.shape, jnp.bfloat16),
        in_specs=[anywhere] * 5 + [scalars] * 2,
        out_specs=anywhere,
        scratch_shapes=[
            pltpu.VMEM((2, tokens, kv_local, width), jnp.bfloat16),
            pltpu.VMEM((2, cache_len, kv_local, width), jnp.bfloat16),
            pltpu.VMEM((2, rows_dev, kv_local, width), jnp.float32),
            pltpu.VMEM((far, 2, rows_dev, width), jnp.bfloat16),
            pltpu.VMEM((far, 2, owners * rows_dev, width), jnp.bfloat16),
            pltpu.VMEM((near, 2, owners * rows_dev, width), jnp.bfloat16),
            pltpu.VMEM((far, tokens, group, width), jnp.bfloat16),
            pltpu.VMEM((near, tokens, group, width), jnp.bfloat16),
            pltpu.VMEM((kv_local, tokens, group, width), jnp.bfloat16),
            pltpu.VMEM((2 * owners, LANES), jnp.int32),
            pltpu.VMEM((2 * owners, LANES), jnp.int32),
            pltpu.VMEM((tokens * group, owners * rows_dev), jnp.float32),
            dma((4,)),
            dma((near,)),
            dma((far, 3 * owners)),
            dma((far, owners)),
            dma((near, 3 * owners)),
            dma((near, owners)),
            dma((2,)),
            dma((2,)),
            dma((far,)),
            dma((far,)),
            dma((near, tokens // TILE_TOKENS)),
            dma((near, tokens // TILE_TOKENS)),
            dma((far,)),
        ],
        compiler_params=pltpu.CompilerParams(
            collective_id=0, has_side_effects=True, vmem_limit_bytes=62 * 1024 * 1024
        ),
    )(queries, span_keys, span_values, cache_keys, cache_values, scale_exps.swapaxes(2, 3), block_order)


def solution(mesh):
    placed = P("pipe", "ctx", "tp", None)
    return jax.shard_map(
        on_device,
        mesh=mesh,
        in_specs=(placed,) * 6 + (P("pipe", None),),
        out_specs=placed,
        check_vma=False,
    )
```

```python
import functools
import math

import jax
import jax.numpy as jnp
from jax import lax
from jax.experimental import pallas as pl
from jax.experimental.pallas import tpu as pltpu
from jax.sharding import PartitionSpec as P

CBLK = 16
LANES = 128
HIDDEN = -1e30
TILE_TOKENS = 16
REACH = 2


def hadamard_signs(order):
    rows = lax.broadcasted_iota(jnp.int32, (order, order), 0)
    both = rows & lax.broadcasted_iota(jnp.int32, (order, order), 1)
    common = jnp.zeros((order, order), jnp.int32)
    for bit in range(order.bit_length() - 1):
        common = common + (jnp.right_shift(both, bit) & 1)
    return (1 - 2 * (common & 1)).astype(jnp.float32).astype(jnp.bfloat16)


def power_of_two(exponent):
    value = jnp.float32(2.0)
    for candidate in range(-3, 1):
        value = jnp.where(exponent == candidate, jnp.float32(2.0**candidate), value)
    return value


def kernel(
    sections, owners, q_ref, sk_ref, sv_ref, ck_ref, cv_ref, exps_ref, order_ref, out_ref,
    raw_span, raw_ctx, wide, stage, kv_far, kv_near, q_far, q_near, mixed, order_near, order_far, bias,
    load_sem, near_sem, far_send, far_recv, near_send, near_recv, pair_send, pair_recv, query_send, query_recv,
    result_send, result_recv, store_sem,
):
    pipe, mine = lax.axis_index("pipe"), lax.axis_index("ctx")
    onward = lax.rem(pipe + 1, sections)
    before = lax.rem(pipe + sections - 1, sections)
    chips = owners // 2
    chip, core = lax.div(mine, 2), lax.rem(mine, 2)
    twin = chip * 2 + 1 - core
    tokens = q_ref.shape[1]
    kv_local = sk_ref.shape[2]
    group = q_ref.shape[2] // kv_local
    width = q_ref.shape[3]
    cache_len = ck_ref.shape[1]
    rows_dev = cache_len + tokens
    half = tokens // 2
    far_heads = kv_far.shape[0]
    near_heads = kv_near.shape[0]
    slot = pl.ds(pl.multiple_of(mine * rows_dev, 16), rows_dev)

    loads = [
        pltpu.make_async_copy(sk_ref.at[0], raw_span.at[0], load_sem.at[0]),
        pltpu.make_async_copy(sv_ref.at[0], raw_span.at[1], load_sem.at[1]),
        pltpu.make_async_copy(ck_ref.at[0], raw_ctx.at[0], load_sem.at[2]),
        pltpu.make_async_copy(cv_ref.at[0], raw_ctx.at[1], load_sem.at[3]),
    ]
    for load in loads:
        load.start()

    def heads(kv_head):
        return pl.ds(kv_head * group, group)

    barrier = pltpu.get_barrier_semaphore()
    pl.semaphore_signal(barrier, inc=1, device_id={"pipe": onward})
    greeted = 2
    if sections > 2:
        pl.semaphore_signal(barrier, inc=1, device_id={"pipe": before})
        greeted = 3
    for distance in range(1, min(REACH, chips - 1) + 1):
        for near_enough in (chip >= distance, chip + distance < chips):
            greeted = greeted + near_enough.astype(jnp.int32)
    pl.semaphore_signal(barrier, inc=1, device_id={"ctx": twin})

    for distance in range(1, min(REACH, chips - 1) + 1):
        for there, other in ((chip >= distance, mine - 2 * distance), (chip + distance < chips, mine + 2 * distance)):

            @pl.when(there)
            def _():
                pl.semaphore_signal(barrier, inc=1, device_id={"ctx": other})

    signs = hadamard_signs(width)
    for block in range(2 * owners):
        order_near[block : block + 1, :] = jnp.full((1, LANES), order_ref[0, block], jnp.int32)


    query_sends = [
        pltpu.make_async_remote_copy(
            q_ref.at[0, :, heads(head), :], q_far.at[head], query_send.at[head], query_recv.at[head],
            device_id={"pipe": onward},
        )
        for head in range(far_heads)
    ]
    near_loads = [
        pltpu.make_async_copy(q_ref.at[0, :, heads(far_heads + head), :], q_near.at[head], near_sem.at[head])
        for head in range(near_heads)
    ]

    for load in loads:
        load.wait()
    for kind in range(2):
        wide[kind, :cache_len] = raw_ctx[kind].astype(jnp.float32)
        wide[kind, cache_len:] = raw_span[kind].astype(jnp.float32)

    def prepared(kv_head, kind):
        rows = wide[kind, :, kv_head, :]
        parts = [
            rows[block * CBLK : (block + 1) * CBLK] * power_of_two(exps_ref[0, block, kind, kv_head])
            for block in range(cache_len // CBLK)
        ]
        rows = jnp.concatenate(parts + [rows[cache_len:]], axis=0).astype(jnp.bfloat16)
        if kind == 1:
            rows = jnp.dot(rows, signs, preferred_element_type=jnp.float32).astype(jnp.bfloat16)
        return rows

    def block_copy(which, head, way, owner, target):
        held = (kv_far, kv_near)[which]
        part = held.at[head, :, pl.ds(pl.multiple_of(owner * rows_dev, 16), rows_dev), :]
        return pltpu.make_async_remote_copy(
            part,
            part,
            (far_send, near_send)[which].at[head, way],
            (far_recv, near_recv)[which].at[head, owner],
            device_id={"ctx": target},
        )

    def others(distance):
        return (
            (chip + distance < chips, mine + 2 * distance, distance),
            (chip >= distance, mine - 2 * distance, chips + distance),
        )

    def send(copy):
        copy.start()

    def sent(copy):
        copy.wait_send()

    def own_head(which, head, act):
        for distance in range(min(REACH, chips - 1), 0, -1):
            for there, other, way in others(distance):

                @pl.when(there)
                def _():
                    act(block_copy(which, head, way, mine, other))

        act(block_copy(which, head, 0, mine, twin))

    def own_block(which, act):
        for head in range((far_heads, near_heads)[which]):
            own_head(which, head, act)

    def step(which, distance, act, waiting):
        ahead = ((chip > 0, mine - 2), (chip < chips - 1, mine + 2))
        for (there, other, way), (further, following) in zip(others(distance), ahead):
            for head in range((far_heads, near_heads)[which]):

                @pl.when(there)
                def _():
                    if waiting:
                        block_copy(which, head, 0, other, twin).wait_recv()

                if distance >= REACH:

                    @pl.when(there & further)
                    def _():
                        act(block_copy(which, head, 4 * chips + way, other, following))

                @pl.when(there)
                def _():
                    act(block_copy(which, head, 2 * chips + way, other, twin))

    def twin_blocks(which):
        for other in range(chips):
            for head in range((far_heads, near_heads)[which]):
                block_copy(which, head, 0, 2 * other + 1 - core, twin).wait_recv()

    for head in range(far_heads):
        for kind in range(2):
            stage[head, kind] = prepared(head, kind)
    for head in range(near_heads):
        for kind in range(2):
            kv_near[head, kind, slot, :] = prepared(far_heads + head, kind)
    pl.semaphore_wait(barrier, greeted)
    pair_sends = [
        pltpu.make_async_remote_copy(
            stage, kv_far.at[:, :, slot, :], pair_send.at[0], pair_recv.at[0], device_id={"pipe": onward}
        ),
        pltpu.make_async_remote_copy(
            order_near, order_far, pair_send.at[1], pair_recv.at[1], device_id={"pipe": onward}
        ),
    ]
    for copy in pair_sends:
        copy.start()
    for copy in query_sends:
        copy.start()
    own_block(1, send)
    for load in near_loads:
        load.start()

    def fill_bias(order):
        token = lax.div(lax.broadcasted_iota(jnp.int32, (tokens * group, LANES), 0), group)
        first = order[pl.ds(2 * mine, 1), :]
        second = order[pl.ds(2 * mine + 1, 1), :]
        place = jnp.where(token < half, first, second) * half + lax.rem(token, half)
        for tile in range(owners * rows_dev // LANES):
            column = tile * LANES + lax.broadcasted_iota(jnp.int32, (1, LANES), 1)
            key_place = jnp.full((1, LANES), -1, jnp.int32)
            for block in range(2 * owners):
                start = (block // 2) * rows_dev + cache_len + (block % 2) * half
                if start < (tile + 1) * LANES and start + half > tile * LANES:
                    inside = (column >= start) & (column < start + half)
                    key_place = jnp.where(inside, order[block : block + 1, :] * half + column - start, key_place)
            bias[:, tile * LANES : (tile + 1) * LANES] = jnp.where(key_place <= place, 0.0, HIDDEN)

    scale = math.log2(math.e) / width**0.5
    shrink = 1.0 / width**0.5
    rows_tile = TILE_TOKENS * group

    def attend(queries, held, head, target, done=None):
        @pl.loop(0, tokens // TILE_TOKENS)
        def _(tile):
            part = pl.ds(pl.multiple_of(tile * TILE_TOKENS, TILE_TOKENS), TILE_TOKENS)
            rows = pl.ds(pl.multiple_of(tile * rows_tile, rows_tile), rows_tile)
            query = queries[head, part].reshape(rows_tile, width)
            score = lax.dot_general(
                query, held[head, 0], (((1,), (1,)), ((), ())), preferred_element_type=jnp.float32
            )
            score = score * scale + bias[rows, :]
            top = jnp.max(score, axis=-1, keepdims=True)
            weight = jnp.exp2(score - top).astype(jnp.bfloat16)
            values = held[head, 1]
            both = jnp.concatenate([values, jnp.ones_like(values)], axis=1)
            total = jnp.dot(weight, both, preferred_element_type=jnp.float32)
            result = total[:, :width] * (shrink / total[:, width:])
            mixed[target, part] = result.astype(jnp.bfloat16).reshape(TILE_TOKENS, group, width)
            if done is not None:
                done(tile)

    fill_bias(order_near)
    if chips > REACH:
        step(1, REACH, send, True)
    pair_sends[0].wait_recv()
    own_block(0, send)
    for distance in list(range(1, min(REACH, chips))) + list(range(REACH + 1, chips)):
        step(1, distance, send, True)
    twin_blocks(1)
    pending = [distance for distance in range(REACH, chips)] + list(range(1, min(REACH, chips)))

    def result_copy(head, tile):
        part = pl.ds(pl.multiple_of(tile * TILE_TOKENS, TILE_TOKENS), TILE_TOKENS)
        return pltpu.make_async_remote_copy(
            mixed.at[far_heads + head, part], out_ref.at[0, part, heads(far_heads + head), :],
            result_send.at[head, tile], result_recv.at[head, tile], device_id={"pipe": onward},
        )

    for head in range(near_heads):
        near_loads[head].wait()
        attend(q_near, kv_near, head, far_heads + head, lambda tile: result_copy(head, tile).start())
        if pending:
            step(0, pending.pop(0), send, True)
    for distance in pending:
        step(0, distance, send, True)
    pair_sends[1].wait_recv()
    fill_bias(order_far)
    twin_blocks(0)
    stores = []
    for head in range(far_heads):
        query_sends[head].wait_recv()
        attend(q_far, kv_far, head, head)
        copy = pltpu.make_async_copy(mixed.at[head], out_ref.at[0, :, heads(head), :], store_sem.at[head])
        copy.start()
        stores.append(copy)

    for which in range(2):
        own_block(which, sent)
        for distance in range(1, chips):
            step(which, distance, sent, False)
    for copy in pair_sends + query_sends:
        copy.wait_send()
    for copy in stores:
        copy.wait()
    for head in range(near_heads):
        for tile in range(tokens // TILE_TOKENS):
            result_copy(head, tile).wait()


def on_device(queries, span_keys, span_values, cache_keys, cache_values, scale_exps, block_order):
    sections, owners = lax.axis_size("pipe"), lax.axis_size("ctx")
    tokens, head_local, width = queries.shape[1:]
    kv_local = span_keys.shape[2]
    group = head_local // kv_local
    cache_len = cache_keys.shape[1]
    rows_dev = cache_len + tokens
    far, near = kv_local // 2, kv_local - kv_local // 2
    anywhere = pl.BlockSpec(memory_space=pl.ANY)
    scalars = pl.BlockSpec(memory_space=pltpu.SMEM)
    dma = pltpu.SemaphoreType.DMA
    return pl.pallas_call(
        functools.partial(kernel, sections, owners),
        out_shape=jax.ShapeDtypeStruct(queries.shape, jnp.bfloat16),
        in_specs=[anywhere] * 5 + [scalars] * 2,
        out_specs=anywhere,
        scratch_shapes=[
            pltpu.VMEM((2, tokens, kv_local, width), jnp.bfloat16),
            pltpu.VMEM((2, cache_len, kv_local, width), jnp.bfloat16),
            pltpu.VMEM((2, rows_dev, kv_local, width), jnp.float32),
            pltpu.VMEM((far, 2, rows_dev, width), jnp.bfloat16),
            pltpu.VMEM((far, 2, owners * rows_dev, width), jnp.bfloat16),
            pltpu.VMEM((near, 2, owners * rows_dev, width), jnp.bfloat16),
            pltpu.VMEM((far, tokens, group, width), jnp.bfloat16),
            pltpu.VMEM((near, tokens, group, width), jnp.bfloat16),
            pltpu.VMEM((kv_local, tokens, group, width), jnp.bfloat16),
            pltpu.VMEM((2 * owners, LANES), jnp.int32),
            pltpu.VMEM((2 * owners, LANES), jnp.int32),
            pltpu.VMEM((tokens * group, owners * rows_dev), jnp.float32),
            dma((4,)),
            dma((near,)),
            dma((far, 3 * owners)),
            dma((far, owners)),
            dma((near, 3 * owners)),
            dma((near, owners)),
            dma((2,)),
            dma((2,)),
            dma((far,)),
            dma((far,)),
            dma((near, tokens // TILE_TOKENS)),
            dma((near, tokens // TILE_TOKENS)),
            dma((far,)),
        ],
        compiler_params=pltpu.CompilerParams(
            collective_id=0, has_side_effects=True, vmem_limit_bytes=62 * 1024 * 1024
        ),
    )(queries, span_keys, span_values, cache_keys, cache_values, scale_exps.swapaxes(2, 3), block_order)


def solution(mesh):
    placed = P("pipe", "ctx", "tp", None)
    return jax.shard_map(
        on_device,
        mesh=mesh,
        in_specs=(placed,) * 6 + (P("pipe", None),),
        out_specs=placed,
        check_vma=False,
    )
```
